32 devices in a mesh: dp: 8 (over z, y), tensor: 4 (over x, core).
Axes of the slice: x: 2, y: 2, z: 4, core: 2. Of those that a mesh axis runs over, the one named last changes fastest.
Arguments:
- cotangent: bfloat16 [2048, 4096], P('dp'), may hold values from -0.375 to 0.375
- activations: bfloat16 [2048, 4096], P('dp', 'tensor'), may hold values from -6 to 6
- error_buf: bfloat16 [8, 4096, 4096], P('dp', None, 'tensor'), may hold values from -6 to 6
- q_start: float32 [32, 4096], P(None, 'tensor'), may hold values from -6 to 6
Outputs:
- basis: float32 [32, 4096], replicated
- q_factor: float32 [32, 4096], P(None, 'tensor')
The draws below stay inside these ranges and needn't reach their ends.
All inputs are finite; a program needn't handle non-finite values.
Results may differ from the reference program's by a relative error of at most 0.0003.
Values sent between devices are 32-bit elements; how exact they have to be, the bound alone decides.
A program may use at most 128 MiB of HBM per device.

```python
import jax
import jax.numpy as jnp
from jax import lax

ROWS = 4096
COLS = 4096
RANK = 32
POWER = 2
TOK_DEV = 256
REPLICAS = 8
TOKENS = 2048


def block_levels(key, dims, cuts, least, high):
    loudness, own = 1.0, jax.random.fold_in(key, 6)
    for axis_at, parts in cuts:
        heights = jnp.exp(jax.random.uniform(jax.random.fold_in(own, axis_at), (parts,), jnp.float32, least / len(cuts), high / len(cuts)))
        loudness = loudness * jnp.repeat(heights, dims[axis_at] // parts).reshape([-1 if axis == axis_at else 1 for axis in range(len(dims))])
    return loudness


def centred(key, dims, spread, limit, split=(), held_as=jnp.bfloat16):
    level = block_levels(key, dims, split, -0.22, 0.18) if split else 1.0
    array = jax.random.normal(key, dims, jnp.float32) * spread * level
    return jnp.minimum(jnp.maximum(array, -limit), limit).astype(held_as)


def setup_inputs(seed: int = 0) -> dict:
    keys = jax.random.split(jax.random.key(seed), 5)
    return {
        "cotangent": centred(keys[0], (TOKENS, ROWS), TOK_DEV ** -0.5, 0.375, ((0, 8),)),
        "activations": centred(keys[1], (TOKENS, COLS), 1.0, 6.0, ((0, 8), (1, 4))),
        "error_buf": centred(keys[2], (REPLICAS, ROWS, COLS), 1.0, 6.0, ((0, 8), (2, 4))),
        "q_start": centred(keys[3], (RANK, COLS), 1.0, 6.0, ((1, 4),), jnp.float32),
    }


def orthonormal(p_sum):
    gram = jnp.dot(p_sum, p_sum.T, precision=lax.Precision.HIGHEST)
    lower = jnp.linalg.cholesky(gram)
    inverse = jax.scipy.linalg.solve_triangular(lower, jnp.eye(RANK, dtype=jnp.float32), lower=True)
    return jnp.dot(inverse, p_sum, precision=lax.Precision.HIGHEST)

def reference(cotangent, activations, error_buf, q_start):
    high = lax.Precision.HIGHEST
    cot_blocks = cotangent.reshape(REPLICAS, TOK_DEV, ROWS)
    act_blocks = activations.reshape(REPLICAS, TOK_DEV, COLS)

    def row_total(q_now):

        def step(total, pieces):
            cot_piece, act_piece, err_piece = pieces
            through = lax.dot_general(q_now, act_piece.astype(jnp.float32), (((1,), (1,)), ((), ())), precision=high)
            term = jnp.dot(through, cot_piece.astype(jnp.float32), precision=high)
            term = term + lax.dot_general(q_now, err_piece.astype(jnp.float32), (((1,), (1,)), ((), ())), precision=high)
            return (total + term, None)
        start = jnp.zeros((RANK, ROWS), jnp.float32)
        return lax.scan(step, start, (cot_blocks, act_blocks, error_buf))[0]

    def col_total(p_hat):

        def step(total, pieces):
            cot_piece, act_piece, err_piece = pieces
            through = lax.dot_general(p_hat, cot_piece.astype(jnp.float32), (((1,), (1,)), ((), ())), precision=high)
            term = jnp.dot(through, act_piece.astype(jnp.float32), precision=high)
            term = term + jnp.dot(p_hat, err_piece.astype(jnp.float32), precision=high)
            return (total + term, None)
        start = jnp.zeros((RANK, COLS), jnp.float32)
        return lax.scan(step, start, (cot_blocks, act_blocks, error_buf))[0]
    q_now = q_start
    p_hat = None
    for number in range(POWER):
        p_hat = orthonormal(row_total(q_now))
        q_now = col_total(p_hat)
    basis = jnp.sqrt(jnp.float32(ROWS)) * p_hat
    return (basis, q_now / REPLICAS)
```

```python
import functools

import jax
import jax.numpy as jnp
from jax import lax
from jax.experimental import pallas as pl
from jax.experimental.pallas import tpu as pltpu
from jax.sharding import PartitionSpec as P

POWER = 2
LANES = 128
NT = (((1,), (1,)), ((), ()))
NN = (((1,), (0,)), ((), ()))
HIGH = lax.Precision.HIGHEST


def lower_inverse(gram):
    lower = jnp.linalg.cholesky(gram)
    return jax.scipy.linalg.solve_triangular(
        lower, jnp.eye(gram.shape[0], dtype=jnp.float32), lower=True
    )


def plain(cotangent, activations, error_buf, q_start):
    carried = error_buf[0]
    gradient = lax.dot_general(
        cotangent, activations, (((0,), (0,)), ((), ())), preferred_element_type=jnp.float32
    )
    fed = gradient + carried.astype(jnp.float32)
    q_now = q_start
    p_hat = None
    for number in range(POWER):
        p_sum = lax.psum(lax.dot_general(q_now, fed, NT, precision=HIGH), ("dp", "tensor"))
        gram = jnp.dot(p_sum, p_sum.T, precision=HIGH)
        p_hat = jnp.dot(lower_inverse(gram), p_sum, precision=HIGH)
        q_now = lax.psum(jnp.dot(p_hat, fed, precision=HIGH), "dp")
    basis = jnp.sqrt(jnp.float32(p_hat.shape[1])) * p_hat
    return (basis, q_now / lax.axis_size("dp"))


def pieces3(x):
    first = x.astype(jnp.bfloat16)
    rest = x - first.astype(jnp.float32)
    second = rest.astype(jnp.bfloat16)
    third = (rest - second.astype(jnp.float32)).astype(jnp.bfloat16)
    return jnp.concatenate([first, second, third], axis=0)


def folded(x):
    n = x.shape[0] // 3
    return (x[2 * n :] + x[n : 2 * n]) + x[:n]


def dot(a, b, dims):
    return lax.dot_general(a, b, dims, preferred_element_type=jnp.float32)


def inverse_factor(gram):
    n = gram.shape[0]
    row = lax.broadcasted_iota(jnp.int32, (n, n), 0)
    column = lax.broadcasted_iota(jnp.int32, (n, n), 1)
    inverse = jnp.where(row == column, 1.0, 0.0).astype(jnp.float32)
    for j in range(n - 1):
        lead = gram[j : j + 1, :]
        ratio = gram[:, j : j + 1] / gram[j : j + 1, j : j + 1]
        factor = jnp.where(row > j, jnp.broadcast_to(ratio, (n, n)), 0.0)
        gram = gram - factor * lead
        inverse = inverse - factor * inverse[j : j + 1, :]
    pivot = jnp.sum(jnp.where(row == column, gram, 0.0), axis=1, keepdims=True)
    root = lax.rsqrt(pivot)
    root = root * (1.5 - 0.5 * ((pivot * root) * root))
    return inverse * root


def kernel(
    replicas, scale,
    cot_hbm, act_hbm, err_hbm, q_hbm, p_out, q_out,
    cot, act, err, q_first, q3,
    send_a, take_a, send_b, take_b, send_c, take_c, full,
    acc, acc_u, acc_g, q_part, q_take, q_full,
    load_sem, a_s, a_r, b_s, b_r, c_s, c_r, d_s, d_r, e_s, e_r, f_s, f_r, g_s, g_r, h_s, h_r,
):
    dp, tensor = lax.axis_index("dp"), lax.axis_index("tensor")
    z, y = dp // 2, dp % 2
    x, core = tensor // 2, tensor % 2
    other = 1 - core
    width = err.shape[2]
    blocks = width // LANES

    def plane(j):
        return (x + j // 2) % 2, (y + j % 2) % 2

    def plane_at(j):
        px, py = plane(j)
        return px * 2 + py

    def plane_device(j):
        px, py = plane(j)
        return (z * 2 + py, px * 2 + core)

    def column_device(k):
        return (((z + k) % 4) * 2 + y, tensor)

    core_device = (dp, x * 2 + other)

    def replica_device(k):
        return ((dp + k) % replicas, tensor)

    order = (1, 2, 3, 0)

    loads = [
        pltpu.make_async_copy(q_hbm, q_first, load_sem.at[0]),
        pltpu.make_async_copy(act_hbm, act, load_sem.at[1]),
        pltpu.make_async_copy(cot_hbm, cot, load_sem.at[2]),
    ]
    err_loads = {}
    for h, half in enumerate((other, core)):
        for n, j in enumerate(order):
            err_loads[h, j] = pltpu.make_async_copy(
                err_hbm.at[half, plane_at(j)], err.at[half, plane_at(j)], load_sem.at[3 + h * 4 + n]
            )
    for copy in loads:
        copy.start()
    for copy in err_loads.values():
        copy.start()

    barrier = pltpu.get_barrier_semaphore()
    partners = [core_device]
    partners += [plane_device(j) for j in (1, 2, 3)]
    partners += [column_device(k) for k in (1, 2, 3)]
    partners += [(((z + k) % 4) * 2 + (1 - y), tensor) for k in (1, 2, 3)]
    for device in partners:
        pl.semaphore_signal(barrier, inc=1, device_id=device, device_id_type=pl.DeviceIdType.MESH)

    def remote(src, dst, send, take, device):
        copy = pltpu.make_async_remote_copy(
            src_ref=src, dst_ref=dst, send_sem=send, recv_sem=take,
            device_id=device, device_id_type=pl.DeviceIdType.MESH,
        )
        copy.start()
        return copy

    for number in range(POWER):
        last = number == POWER - 1
        if number == 0:
            loads[0].wait()
            q_now = q_first[...]
        else:
            q_now = jnp.concatenate([q_full[i] for i in range(replicas)], axis=1)
        q3[...] = pieces3(q_now)
        if number == 0:
            loads[1].wait()
        through3 = pieces3(folded(dot(q3[...], act[...], NT)))
        if number == 0:
            loads[2].wait()

        def row_term(h, half, j):
            at = plane_at(j)
            if number == 0:
                err_loads[h, j].wait()
            columns = pl.ds(pl.multiple_of((half * 4 + at) * width, width), width)
            return folded(
                dot(q3[...], err[half, at], NT) + dot(through3, cot[:, columns], NN)
            )

        sends = []
        core_sums = {}
        for j in order:
            term = row_term(0, other, j)
            for b in range(blocks):
                send_a[j, b] = term[:, b * LANES : (b + 1) * LANES]
            if number == 0 and j == order[0]:
                pl.semaphore_wait(barrier, len(partners))
            core_sums[j] = remote(send_a.at[j], take_a.at[j], a_s.at[j], a_r.at[j], core_device)
        sends += list(core_sums.values())
        plane_sums = {}
        for j in order:
            term = row_term(1, core, j)
            core_sums[j].wait_recv()
            for b in range(blocks):
                send_b[j, b] = term[:, b * LANES : (b + 1) * LANES] + take_a[j, b]
            if j:
                plane_sums[j] = remote(send_b.at[j], take_b.at[j], b_s.at[j], b_r.at[j], plane_device(j))
        sends += list(plane_sums.values())
        for j in (1, 2, 3):
            plane_sums[j].wait_recv()
        for b in range(blocks):
            send_c[b] = (send_b[0, b] + take_b[1, b]) + (take_b[2, b] + take_b[3, b])
        column_sums = [
            remote(send_c.at[(z + k) % 4], take_c.at[k], c_s.at[k], c_r.at[k], column_device(k))
            for k in (1, 2, 3)
        ]
        sends += column_sums
        for copy in column_sums:
            copy.wait_recv()
        mine = plane_at(0)
        full[core, mine, z] = (send_c[z] + take_c[1]) + (take_c[2] + take_c[3])

        block = full.at[core, mine, z]
        column_full = [
            remote(block, block, d_s.at[k], d_r.at[k], column_device(k)) for k in (1, 2, 3)
        ]
        sends += column_full
        for copy in column_full:
            copy.wait_recv()
        piece = full.at[core, mine]
        plane_full = {
            j: remote(piece, piece, e_s.at[j], e_r.at[j], plane_device(j)) for j in (1, 2, 3)
        }
        sends += list(plane_full.values())
        core_full = {0: remote(piece, piece, f_s.at[0], f_r.at[0], core_device)}

        def column_term(half, j, first):
            at = plane_at(j)
            p3 = pieces3(jnp.concatenate([full[half, at, b] for b in range(blocks)], axis=1))
            columns = pl.ds(pl.multiple_of((half * 4 + at) * width, width), width)
            by_err = dot(p3, err[half, at], NN)
            by_cot = dot(p3, cot[:, columns], NT)
            by_self = dot(p3, p3, NT)
            if first:
                acc[...] = by_err
                acc_u[...] = by_cot
                acc_g[...] = by_self
            else:
                acc[...] += by_err
                acc_u[...] += by_cot
                acc_g[...] += by_self

        column_term(core, 0, True)
        for j in (1, 2, 3):
            plane_full[j].wait_recv()
            got = full.at[core, plane_at(j)]
            core_full[j] = remote(got, got, f_s.at[j], f_r.at[j], core_device)
            column_term(core, j, False)
        for j in range(4):
            core_full[j].wait_recv()
            column_term(other, j, False)
        sends += list(core_full.values())

        q_sum = folded(acc[...]) + folded(dot(pieces3(folded(acc_u[...])), act[...], NN))
        for i in range(replicas):
            q_part[i] = q_sum[:, i * LANES : (i + 1) * LANES]
        q_sums = [
            remote(q_part.at[(dp + k) % replicas], q_take.at[k], g_s.at[k], g_r.at[k], replica_device(k))
            for k in range(1, replicas)
        ]
        sends += q_sums
        rank = q_sum.shape[0]
        g_rows = folded(acc_g[...])
        gram = (g_rows[:, 2 * rank :] + g_rows[:, rank : 2 * rank]) + g_rows[:, :rank]
        inverse = inverse_factor(gram)
        total = q_part[dp]
        for k, copy in enumerate(q_sums):
            copy.wait_recv()
            total = total + q_take[k + 1]
        q_own = jnp.dot(inverse, total, precision=HIGH, preferred_element_type=jnp.float32)
        if last:
            q_own = q_own / replicas
        q_full[dp] = q_own
        q_back = [
            remote(q_full.at[dp], q_full.at[dp], h_s.at[k], h_r.at[k], replica_device(k))
            for k in range(1, replicas)
        ]
        sends += q_back
        if last:
            for half in range(2):
                for at in range(4):
                    p_sum = jnp.concatenate([full[half, at, b] for b in range(blocks)], axis=1)
                    p_hat = jnp.dot(inverse, p_sum, precision=HIGH, preferred_element_type=jnp.float32)
                    start = (half * 4 + at) * width
                    p_out[:, start : start + width] = p_hat * scale
        for copy in q_back:
            copy.wait_recv()
        if last:
            for i in range(replicas):
                q_out[:, i * LANES : (i + 1) * LANES] = q_full[i]
        for copy in sends:
            copy.wait_send()


def fits(replicas, shards, tokens, rows, columns, rank):
    return replicas == 8 and shards == 4 and rows == 32 * LANES and columns == replicas * LANES and rank % 16 == 0


def solution(mesh):
    replicas, shards = mesh.shape["dp"], mesh.shape["tensor"]

    def on_device(cotangent, activations, error_buf, q_start):
        tokens, rows = cotangent.shape
        rank, columns = q_start.shape
        if not fits(replicas, shards, tokens, rows, columns, rank):
            return plain(cotangent, activations, error_buf, q_start)
        width = rows // 8
        blocks = width // LANES
        f32 = jnp.float32
        dma = pltpu.SemaphoreType.DMA
        any_space = pl.BlockSpec(memory_space=pl.ANY)
        vmem = pl.BlockSpec(memory_space=pltpu.VMEM)
        sems = [dma((11,))]
        for count in (4, 4, 4, 4, 4, 4, replicas, replicas):
            sems += [dma((count,)), dma((count,))]
        return pl.pallas_call(
            functools.partial(kernel, replicas, float(rows) ** 0.5),
            out_shape=(
                jax.ShapeDtypeStruct((rank, rows), f32),
                jax.ShapeDtypeStruct((rank, columns), f32),
            ),
            in_specs=[any_space] * 4,
            out_specs=(vmem, vmem),
            scratch_shapes=[
                pltpu.VMEM((tokens, rows), jnp.bfloat16),
                pltpu.VMEM((tokens, columns), jnp.bfloat16),
                pltpu.VMEM((2, 4, width, columns), jnp.bfloat16),
                pltpu.VMEM((rank, columns), f32),
                pltpu.VMEM((3 * rank, columns), jnp.bfloat16),
                pltpu.VMEM((4, blocks, rank, LANES), f32),
                pltpu.VMEM((4, blocks, rank, LANES), f32),
                pltpu.VMEM((4, blocks, rank, LANES), f32),
                pltpu.VMEM((4, blocks, rank, LANES), f32),
                pltpu.VMEM((blocks, rank, LANES), f32),
                pltpu.VMEM((4, rank, LANES), f32),
                pltpu.VMEM((2, 4, blocks, rank, LANES), f32),
                pltpu.VMEM((3 * rank, columns), f32),
                pltpu.VMEM((3 * rank, tokens), f32),
                pltpu.VMEM((3 * rank, 3 * rank), f32),
                pltpu.VMEM((replicas, rank, LANES), f32),
                pltpu.VMEM((replicas, rank, LANES), f32),
                pltpu.VMEM((replicas, rank, LANES), f32),
            ]
            + sems,
            compiler_params=pltpu.CompilerParams(
                collective_id=0, has_side_effects=True, vmem_limit_bytes=48 * 1024 * 1024
            ),
        )(cotangent, activations, error_buf.reshape(2, 4, width, columns), q_start)

    return jax.shard_map(
        on_device,
        mesh=mesh,
        in_specs=(P("dp", None), P("dp", "tensor"), P("dp", None, "tensor"), P(None, "tensor")),
        out_specs=(P(), P(None, "tensor")),
        check_vma=False,
    )
```

```python
import functools

import jax
import jax.numpy as jnp
from jax import lax
from jax.experimental import pallas as pl
from jax.experimental.pallas import tpu as pltpu
from jax.sharding import PartitionSpec as P

POWER = 2
LANES = 128
NT = (((1,), (1,)), ((), ()))
NN = (((1,), (0,)), ((), ()))
HIGH = lax.Precision.HIGHEST


def lower_inverse(gram):
    lower = jnp.linalg.cholesky(gram)
    return jax.scipy.linalg.solve_triangular(
        lower, jnp.eye(gram.shape[0], dtype=jnp.float32), lower=True
    )


def plain(cotangent, activations, error_buf, q_start):
    carried = error_buf[0]
    gradient = lax.dot_general(
        cotangent, activations, (((0,), (0,)), ((), ())), preferred_element_type=jnp.float32
    )
    fed = gradient + carried.astype(jnp.float32)
    q_now = q_start
    p_hat = None
    for number in range(POWER):
        p_sum = lax.psum(lax.dot_general(q_now, fed, NT, precision=HIGH), ("dp", "tensor"))
        gram = jnp.dot(p_sum, p_sum.T, precision=HIGH)
        p_hat = jnp.dot(lower_inverse(gram), p_sum, precision=HIGH)
        q_now = lax.psum(jnp.dot(p_hat, fed, precision=HIGH), "dp")
    basis = jnp.sqrt(jnp.float32(p_hat.shape[1])) * p_hat
    return (basis, q_now / lax.axis_size("dp"))


def pieces3(x):
    first = x.astype(jnp.bfloat16)
    rest = x - first.astype(jnp.float32)
    second = rest.astype(jnp.bfloat16)
    third = (rest - second.astype(jnp.float32)).astype(jnp.bfloat16)
    return jnp.concatenate([first, second, third], axis=0)


def folded(x):
    n = x.shape[0] // 3
    return (x[2 * n :] + x[n : 2 * n]) + x[:n]


def dot(a, b, dims):
    return lax.dot_general(a, b, dims, preferred_element_type=jnp.float32)


def inverse_factor(gram):
    n = gram.shape[0]
    row = lax.broadcasted_iota(jnp.int32, (n, n), 0)
    column = lax.broadcasted_iota(jnp.int32, (n, n), 1)
    inverse = jnp.where(row == column, 1.0, 0.0).astype(jnp.float32)
    for j in range(n - 1):
        lead = gram[j : j + 1, :]
        ratio = gram[:, j : j + 1] / gram[j : j + 1, j : j + 1]
        factor = jnp.where(row > j, jnp.broadcast_to(ratio, (n, n)), 0.0)
        gram = gram - factor * lead
        inverse = inverse - factor * inverse[j : j + 1, :]
    pivot = jnp.sum(jnp.where(row == column, gram, 0.0), axis=1, keepdims=True)
    root = lax.rsqrt(pivot)
    root = root * (1.5 - 0.5 * ((pivot * root) * root))
    return inverse * root


def kernel(
    replicas, scale,
    cot_hbm, act_hbm, err_hbm, q_hbm, p_out, q_out,
    cot, act, err, q_first, q3,
    send_a, take_a, send_b, take_b, full,
    acc, acc_u, acc_g, q_part, q_take, q_full,
    load_sem, a_s, a_r, b_s, b_r, c_s, c_r, f_s, f_r, g_s, g_r, h_s, h_r,
):
    dp, tensor = lax.axis_index("dp"), lax.axis_index("tensor")
    z, y = dp // 2, dp % 2
    x, core = tensor // 2, tensor % 2
    other = 1 - core
    width = err.shape[2]
    blocks = width // LANES

    def plane(j):
        return (x + j // 2) % 2, (y + j % 2) % 2

    def plane_at(j):
        px, py = plane(j)
        return px * 2 + py

    def chip_device(j, k):
        px, py = plane(j)
        return (((z + k) % 4) * 2 + py, px * 2 + core)

    core_device = (dp, x * 2 + other)

    def replica_device(k):
        return ((dp + k) % replicas, tensor)

    order = (1, 2, 3, 0)
    far = (2, 1, 3, 0)

    loads = [
        pltpu.make_async_copy(q_hbm, q_first, load_sem.at[0]),
        pltpu.make_async_copy(act_hbm, act, load_sem.at[1]),
        pltpu.make_async_copy(cot_hbm, cot, load_sem.at[2]),
    ]
    err_loads = {}
    for h, half in enumerate((other, core)):
        for n, j in enumerate(order):
            err_loads[h, j] = pltpu.make_async_copy(
                err_hbm.at[half, plane_at(j)], err.at[half, plane_at(j)], load_sem.at[3 + h * 4 + n]
            )
    for copy in loads:
        copy.start()
    for copy in err_loads.values():
        copy.start()

    barrier = pltpu.get_barrier_semaphore()
    partners = [core_device]
    partners += [chip_device(j, k) for j in range(4) for k in range(4) if j or k]
    for device in partners:
        pl.semaphore_signal(barrier, inc=1, device_id=device, device_id_type=pl.DeviceIdType.MESH)

    def remote(src, dst, send, take, device):
        copy = pltpu.make_async_remote_copy(
            src_ref=src, dst_ref=dst, send_sem=send, recv_sem=take,
            device_id=device, device_id_type=pl.DeviceIdType.MESH,
        )
        copy.start()
        return copy

    for number in range(POWER):
        last = number == POWER - 1
        if number == 0:
            loads[0].wait()
            q_now = q_first[...]
        else:
            q_now = jnp.concatenate([q_full[i] for i in range(replicas)], axis=1)
        q3[...] = pieces3(q_now)
        if number == 0:
            loads[1].wait()
        through3 = pieces3(folded(dot(q3[...], act[...], NT)))
        if number == 0:
            loads[2].wait()

        def row_term(h, half, j):
            at = plane_at(j)
            if number == 0:
                err_loads[h, j].wait()
            columns = pl.ds(pl.multiple_of((half * 4 + at) * width, width), width)
            return folded(
                dot(q3[...], err[half, at], NT) + dot(through3, cot[:, columns], NN)
            )

        sends = []
        core_sums = {}
        for j in order:
            term = row_term(0, other, j)
            for b in range(blocks):
                send_a[j, b] = term[:, b * LANES : (b + 1) * LANES]
            if number == 0 and j == order[0]:
                pl.semaphore_wait(barrier, len(partners))
            core_sums[j] = remote(send_a.at[j], take_a.at[j], a_s.at[j], a_r.at[j], core_device)
        sends += list(core_sums.values())
        chip_sums = []
        for j in order:
            term = row_term(1, core, j)
            core_sums[j].wait_recv()
            for b in range(blocks):
                send_b[j, b] = term[:, b * LANES : (b + 1) * LANES] + take_a[j, b]
            for k in far:
                if j or k:
                    n = j * 4 + k
                    chip_sums.append(
                        remote(send_b.at[j, (z + k) % 4], take_b.at[n], b_s.at[n], b_r.at[n], chip_device(j, k))
                    )
        sends += chip_sums
        mine = plane_at(0)
        total = send_b[0, z]
        for copy in chip_sums:
            copy.wait_recv()
        for n in range(1, 16):
            total = total + take_b[n]
        full[core, mine, z] = total

        block = full.at[core, mine, z]
        chip_full = {}
        for j in (0, 1, 2, 3):
            for k in far:
                if j or k:
                    n = j * 4 + k
                    chip_full[j, k] = remote(block, block, c_s.at[n], c_r.at[n], chip_device(j, k))
        sends += list(chip_full.values())
        core_full = {}

        def column_term(half, j, first):
            at = plane_at(j)
            p3 = pieces3(jnp.concatenate([full[half, at, b] for b in range(blocks)], axis=1))
            columns = pl.ds(pl.multiple_of((half * 4 + at) * width, width), width)
            by_err = dot(p3, err[half, at], NN)
            by_cot = dot(p3, cot[:, columns], NT)
            by_self = dot(p3, p3, NT)
            if first:
                acc[...] = by_err
                acc_u[...] = by_cot
                acc_g[...] = by_self
            else:
                acc[...] += by_err
                acc_u[...] += by_cot
                acc_g[...] += by_self

        for j in range(4):
            for k in far:
                if j or k:
                    chip_full[j, k].wait_recv()
            got = full.at[core, plane_at(j)]
            core_full[j] = remote(got, got, f_s.at[j], f_r.at[j], core_device)
            column_term(core, j, j == 0)
        for j in range(4):
            core_full[j].wait_recv()
            column_term(other, j, False)
        sends += list(core_full.values())

        q_sum = folded(acc[...]) + folded(dot(pieces3(folded(acc_u[...])), act[...], NN))
        for i in range(replicas):
            q_part[i] = q_sum[:, i * LANES : (i + 1) * LANES]
        q_sums = [
            remote(q_part.at[(dp + k) % replicas], q_take.at[k], g_s.at[k], g_r.at[k], replica_device(k))
            for k in range(1, replicas)
        ]
        sends += q_sums
        rank = q_sum.shape[0]
        g_rows = folded(acc_g[...])
        gram = (g_rows[:, 2 * rank :] + g_rows[:, rank : 2 * rank]) + g_rows[:, :rank]
        inverse = inverse_factor(gram)
        total = q_part[dp]
        for k, copy in enumerate(q_sums):
            copy.wait_recv()
            total = total + q_take[k + 1]
        q_own = jnp.dot(inverse, total, precision=HIGH, preferred_element_type=jnp.float32)
        if last:
            q_own = q_own / replicas
        q_full[dp] = q_own
        q_back = [
            remote(q_full.at[dp], q_full.at[dp], h_s.at[k], h_r.at[k], replica_device(k))
            for k in range(1, replicas)
        ]
        sends += q_back
        if last:
            for half in range(2):
                for at in range(4):
                    p_sum = jnp.concatenate([full[half, at, b] for b in range(blocks)], axis=1)
                    p_hat = jnp.dot(inverse, p_sum, precision=HIGH, preferred_element_type=jnp.float32)
                    start = (half * 4 + at) * width
                    p_out[:, start : start + width] = p_hat * scale
        for copy in q_back:
            copy.wait_recv()
        if last:
            for i in range(replicas):
                q_out[:, i * LANES : (i + 1) * LANES] = q_full[i]
        for copy in sends:
            copy.wait_send()


def fits(replicas, shards, tokens, rows, columns, rank):
    return replicas == 8 and shards == 4 and rows == 32 * LANES and columns == replicas * LANES and rank % 16 == 0


def solution(mesh):
    replicas, shards = mesh.shape["dp"], mesh.shape["tensor"]

    def on_device(cotangent, activations, error_buf, q_start):
        tokens, rows = cotangent.shape
        rank, columns = q_start.shape
        if not fits(replicas, shards, tokens, rows, columns, rank):
            return plain(cotangent, activations, error_buf, q_start)
        width = rows // 8
        blocks = width // LANES
        f32 = jnp.float32
        dma = pltpu.SemaphoreType.DMA
        any_space = pl.BlockSpec(memory_space=pl.ANY)
        vmem = pl.BlockSpec(memory_space=pltpu.VMEM)
        sems = [dma((11,))]
        for count in (4, 16, 16, 4, replicas, replicas):
            sems += [dma((count,)), dma((count,))]
        return pl.pallas_call(
            functools.partial(kernel, replicas, float(rows) ** 0.5),
            out_shape=(
                jax.ShapeDtypeStruct((rank, rows), f32),
                jax.ShapeDtypeStruct((rank, columns), f32),
            ),
            in_specs=[any_space] * 4,
            out_specs=(vmem, vmem),
            scratch_shapes=[
                pltpu.VMEM((tokens, rows), jnp.bfloat16),
                pltpu.VMEM((tokens, columns), jnp.bfloat16),
                pltpu.VMEM((2, 4, width, columns), jnp.bfloat16),
                pltpu.VMEM((rank, columns), f32),
                pltpu.VMEM((3 * rank, columns), jnp.bfloat16),
                pltpu.VMEM((4, blocks, rank, LANES), f32),
                pltpu.VMEM((4, blocks, rank, LANES), f32),
                pltpu.VMEM((4, blocks, rank, LANES), f32),
                pltpu.VMEM((16, rank, LANES), f32),
                pltpu.VMEM((2, 4, blocks, rank, LANES), f32),
                pltpu.VMEM((3 * rank, columns), f32),
                pltpu.VMEM((3 * rank, tokens), f32),
                pltpu.VMEM((3 * rank, 3 * rank), f32),
                pltpu.VMEM((replicas, rank, LANES), f32),
                pltpu.VMEM((replicas, rank, LANES), f32),
                pltpu.VMEM((replicas, rank, LANES), f32),
            ]
            + sems,
            compiler_params=pltpu.CompilerParams(
                collective_id=0, has_side_effects=True, vmem_limit_bytes=60 * 1024 * 1024
            ),
        )(cotangent, activations, error_buf.reshape(2, 4, width, columns), q_start)

    return jax.shard_map(
        on_device,
        mesh=mesh,
        in_specs=(P("dp", None), P("dp", "tensor"), P("dp", None, "tensor"), P(None, "tensor")),
        out_specs=(P(), P(None, "tensor")),
        check_vma=False,
    )
```

```python
import functools

import jax
import jax.numpy as jnp
from jax import lax
from jax.experimental import pallas as pl
from jax.experimental.pallas import tpu as pltpu
from jax.sharding import PartitionSpec as P

POWER = 2
LANES = 128
NT = (((1,), (1,)), ((), ()))
NN = (((1,), (0,)), ((), ()))
HIGH = lax.Precision.HIGHEST


def lower_inverse(gram):
    lower = jnp.linalg.cholesky(gram)
    return jax.scipy.linalg.solve_triangular(
        lower, jnp.eye(gram.shape[0], dtype=jnp.float32), lower=True
    )


def plain(cotangent, activations, error_buf, q_start):
    carried = error_buf[0]
    gradient = lax.dot_general(
        cotangent, activations, (((0,), (0,)), ((), ())), preferred_element_type=jnp.float32
    )
    fed = gradient + carried.astype(jnp.float32)
    q_now = q_start
    p_hat = None
    for number in range(POWER):
        p_sum = lax.psum(lax.dot_general(q_now, fed, NT, precision=HIGH), ("dp", "tensor"))
        gram = jnp.dot(p_sum, p_sum.T, precision=HIGH)
        p_hat = jnp.dot(lower_inverse(gram), p_sum, precision=HIGH)
        q_now = lax.psum(jnp.dot(p_hat, fed, precision=HIGH), "dp")
    basis = jnp.sqrt(jnp.float32(p_hat.shape[1])) * p_hat
    return (basis, q_now / lax.axis_size("dp"))


def pieces3(x):
    first = x.astype(jnp.bfloat16)
    rest = x - first.astype(jnp.float32)
    second = rest.astype(jnp.bfloat16)
    third = (rest - second.astype(jnp.float32)).astype(jnp.bfloat16)
    return jnp.concatenate([first, second, third], axis=0)


def folded(x):
    n = x.shape[0] // 3
    return (x[2 * n :] + x[n : 2 * n]) + x[:n]


def dot(a, b, dims):
    return lax.dot_general(a, b, dims, preferred_element_type=jnp.float32)


def inverse_factor(gram):
    n = gram.shape[0]
    row = lax.broadcasted_iota(jnp.int32, (n, n), 0)
    column = lax.broadcasted_iota(jnp.int32, (n, n), 1)
    inverse = jnp.where(row == column, 1.0, 0.0).astype(jnp.float32)
    for j in range(n - 1):
        lead = gram[j : j + 1, :]
        ratio = gram[:, j : j + 1] / gram[j : j + 1, j : j + 1]
        factor = jnp.where(row > j, jnp.broadcast_to(ratio, (n, n)), 0.0)
        gram = gram - factor * lead
        inverse = inverse - factor * inverse[j : j + 1, :]
    pivot = jnp.sum(jnp.where(row == column, gram, 0.0), axis=1, keepdims=True)
    root = lax.rsqrt(pivot)
    root = root * (1.5 - 0.5 * ((pivot * root) * root))
    return inverse * root


def kernel(
    replicas, scale,
    cot_hbm, act_hbm, err_hbm, q_hbm, p_out, q_out,
    cot, act, err, q_first, q3,
    send_a, take_a, send_b, take_b, full,
    acc, acc_u, acc_g, q_part, q_take, q_full,
    load_sem, a_s, a_r, b_s, b_r, c_s, c_r, f_s, f_r, g_s, g_r, h_s, h_r,
):
    dp, tensor = lax.axis_index("dp"), lax.axis_index("tensor")
    z, y = dp // 2, dp % 2
    x, core = tensor // 2, tensor % 2
    other = 1 - core
    width = err.shape[2]
    blocks = width // LANES

    def plane(j):
        return (x + j // 2) % 2, (y + j % 2) % 2

    def plane_at(j):
        px, py = plane(j)
        return px * 2 + py

    def chip_device(j, k):
        px, py = plane(j)
        return (((z + k) % 4) * 2 + py, px * 2 + core)

    core_device = (dp, x * 2 + other)

    def replica_device(k):
        return ((dp + k) % replicas, tensor)

    order = (1, 2, 3, 0)
    far = (2, 1, 3, 0)

    loads = [
        pltpu.make_async_copy(q_hbm, q_first, load_sem.at[0]),
        pltpu.make_async_copy(act_hbm, act, load_sem.at[1]),
        pltpu.make_async_copy(cot_hbm, cot, load_sem.at[2]),
    ]
    err_loads = {}
    for h, half in enumerate((other, core)):
        for n, j in enumerate(order):
            err_loads[h, j] = pltpu.make_async_copy(
                err_hbm.at[half, plane_at(j)], err.at[half, plane_at(j)], load_sem.at[3 + h * 4 + n]
            )
    for copy in loads:
        copy.start()
    for copy in err_loads.values():
        copy.start()

    barrier = pltpu.get_barrier_semaphore()
    partners = [core_device]
    partners += [chip_device(j, k) for j in range(4) for k in range(4) if j or k]
    for device in partners:
        pl.semaphore_signal(barrier, inc=1, device_id=device, device_id_type=pl.DeviceIdType.MESH)

    def remote(src, dst, send, take, device):
        copy = pltpu.make_async_remote_copy(
            src_ref=src, dst_ref=dst, send_sem=send, recv_sem=take,
            device_id=device, device_id_type=pl.DeviceIdType.MESH,
        )
        copy.start()
        return copy

    for number in range(POWER):
        last = number == POWER - 1
        if number == 0:
            loads[0].wait()
            q_now = q_first[...]
        else:
            q_now = jnp.concatenate([q_full[i] for i in range(replicas)], axis=1)
        q3[...] = pieces3(q_now)
        if number == 0:
            loads[1].wait()
        through3 = pieces3(folded(dot(q3[...], act[...], NT)))
        if number == 0:
            loads[2].wait()

        def row_term(h, half, j):
            at = plane_at(j)
            if number == 0:
                err_loads[h, j].wait()
            columns = pl.ds(pl.multiple_of((half * 4 + at) * width, width), width)
            return folded(
                dot(q3[...], err[half, at], NT) + dot(through3, cot[:, columns], NN)
            )

        sends = []
        core_sums = {}
        for j in order:
            term = row_term(0, other, j)
            for b in range(blocks):
                send_a[j, b] = term[:, b * LANES : (b + 1) * LANES]
            if number == 0 and j == order[0]:
                pl.semaphore_wait(barrier, len(partners))
            core_sums[j] = remote(send_a.at[j], take_a.at[j], a_s.at[j], a_r.at[j], core_device)
        sends += list(core_sums.values())
        chip_sums = []
        for j in order:
            term = row_term(1, core, j)
            core_sums[j].wait_recv()
            for b in range(blocks):
                send_b[j, b] = term[:, b * LANES : (b + 1) * LANES] + take_a[j, b]
            for k in far:
                if j or k:
                    n = j * 4 + k
                    chip_sums.append(
                        remote(send_b.at[j, (z + k) % 4], take_b.at[n], b_s.at[n], b_r.at[n], chip_device(j, k))
                    )
        sends += chip_sums
        mine = plane_at(0)
        total = send_b[0, z]
        for copy in chip_sums:
            copy.wait_recv()
        for n in range(1, 16):
            total = total + take_b[n]
        full[core, mine, z] = total

        block = full.at[core, mine, z]
        chip_full = {}
        for j in (0, 1, 2, 3):
            for k in far:
                if j or k:
                    n = j * 4 + k
                    chip_full[j, k] = remote(block, block, c_s.at[n], c_r.at[n], chip_device(j, k))
        sends += list(chip_full.values())
        core_full = {}

        def column_term(half, j, first):
            at = plane_at(j)
            p3 = pieces3(jnp.concatenate([full[half, at, b] for b in range(blocks)], axis=1))
            columns = pl.ds(pl.multiple_of((half * 4 + at) * width, width), width)
            by_err = dot(p3, err[half, at], NN)
            by_cot = dot(p3, cot[:, columns], NT)
            by_self = dot(p3, p3, NT)
            if first:
                acc[...] = by_err
                acc_u[...] = by_cot
                acc_g[...] = by_self
            else:
                acc[...] += by_err
                acc_u[...] += by_cot
                acc_g[...] += by_self

        for j in range(4):
            for k in far:
                if j or k:
                    chip_full[j, k].wait_recv()
            got = full.at[core, plane_at(j)]
            core_full[j] = remote(got, got, f_s.at[j], f_r.at[j], core_device)
            column_term(core, j, j == 0)
        for j in range(4):
            core_full[j].wait_recv()
            column_term(other, j, False)
        sends += list(core_full.values())

        q_sum = folded(acc[...]) + folded(dot(pieces3(folded(acc_u[...])), act[...], NN))
        for i in range(replicas):
            q_part[i] = q_sum[:, i * LANES : (i + 1) * LANES]
        q_sums = [
            remote(q_part.at[(dp + k) % replicas], q_take.at[k], g_s.at[k], g_r.at[k], replica_device(k))
            for k in range(1, replicas)
        ]
        sends += q_sums
        rank = q_sum.shape[0]
        g_rows = folded(acc_g[...])
        gram = (g_rows[:, 2 * rank :] + g_rows[:, rank : 2 * rank]) + g_rows[:, :rank]
        inverse = inverse_factor(gram)
        total = q_part[dp]
        for k, copy in enumerate(q_sums):
            copy.wait_recv()
            total = total + q_take[k + 1]
        q_own = jnp.dot(inverse, total, precision=HIGH, preferred_element_type=jnp.float32)
        if last:
            q_own = q_own / replicas
        q_full[dp] = q_own
        q_back = [
            remote(q_full.at[dp], q_full.at[dp], h_s.at[k], h_r.at[k], replica_device(k))
            for k in range(1, replicas)
        ]
        sends += q_back
        if last:
            for half in range(2):
                for at in range(4):
                    p_sum = jnp.concatenate([full[half, at, b] for b in range(blocks)], axis=1)
                    p_hat = jnp.dot(inverse, p_sum, precision=HIGH, preferred_element_type=jnp.float32)
                    start = (half * 4 + at) * width
                    p_out[:, start : start + width] = p_hat * scale
        for copy in q_back:
            copy.wait_recv()
        if last:
            for i in range(replicas):
                q_out[:, i * LANES : (i + 1) * LANES] = q_full[i]
        for copy in sends:
            copy.wait_send()


def hand_out(p_in, q_in, p_out, q_out):
    p_out[...] = p_in[...]
    q_out[...] = q_in[...]


def fits(replicas, shards, tokens, rows, columns, rank):
    return replicas == 8 and shards == 4 and rows == 32 * LANES and columns == replicas * LANES and rank % 16 == 0


def solution(mesh):
    replicas, shards = mesh.shape["dp"], mesh.shape["tensor"]

    def on_device(cotangent, activations, error_buf, q_start):
        tokens, rows = cotangent.shape
        rank, columns = q_start.shape
        if not fits(replicas, shards, tokens, rows, columns, rank):
            return plain(cotangent, activations, error_buf, q_start)
        width = rows // 8
        blocks = width // LANES
        f32 = jnp.float32
        dma = pltpu.SemaphoreType.DMA
        any_space = pl.BlockSpec(memory_space=pl.ANY)
        vmem = pl.BlockSpec(memory_space=pltpu.VMEM)
        sems = [dma((11,))]
        for count in (4, 16, 16, 4, replicas, replicas):
            sems += [dma((count,)), dma((count,))]
        shapes = (
            jax.ShapeDtypeStruct((rank, rows), f32),
            jax.ShapeDtypeStruct((rank, columns), f32),
        )
        found = pl.pallas_call(
            functools.partial(kernel, replicas, float(rows) ** 0.5),
            out_shape=shapes,
            in_specs=[any_space] * 4,
            out_specs=(vmem, vmem),
            scratch_shapes=[
                pltpu.VMEM((tokens, rows), jnp.bfloat16),
                pltpu.VMEM((tokens, columns), jnp.bfloat16),
                pltpu.VMEM((2, 4, width, columns), jnp.bfloat16),
                pltpu.VMEM((rank, columns), f32),
                pltpu.VMEM((3 * rank, columns), jnp.bfloat16),
                pltpu.VMEM((4, blocks, rank, LANES), f32),
                pltpu.VMEM((4, blocks, rank, LANES), f32),
                pltpu.VMEM((4, blocks, rank, LANES), f32),
                pltpu.VMEM((16, rank, LANES), f32),
                pltpu.VMEM((2, 4, blocks, rank, LANES), f32),
                pltpu.VMEM((3 * rank, columns), f32),
                pltpu.VMEM((3 * rank, tokens), f32),
                pltpu.VMEM((3 * rank, 3 * rank), f32),
                pltpu.VMEM((replicas, rank, LANES), f32),
                pltpu.VMEM((replicas, rank, LANES), f32),
                pltpu.VMEM((replicas, rank, LANES), f32),
            ]
            + sems,
            compiler_params=pltpu.CompilerParams(
                collective_id=0, has_side_effects=True, vmem_limit_bytes=60 * 1024 * 1024
            ),
        )(cotangent, activations, error_buf.reshape(2, 4, width, columns), q_start)
        return pl.pallas_call(
            hand_out,
            out_shape=shapes,
            in_specs=[vmem] * 2,
            out_specs=(vmem, vmem),
        )(*found)

    return jax.shard_map(
        on_device,
        mesh=mesh,
        in_specs=(P("dp", None), P("dp", "tensor"), P("dp", None, "tensor"), P(None, "tensor")),
        out_specs=(P(), P(None, "tensor")),
        check_vma=False,
    )
```
